32 devices in a mesh: section: 4 (over x, core), row: 8 (over z, y).
Axes of the slice: x: 2, y: 2, z: 4, core: 2. Of those that a mesh axis runs over, the one named last changes fastest.
Arguments:
- pair_in: bfloat16 [4, 256, 256, 128], P('section', 'row'), may hold values from -6 to 6
- upstream: bfloat16 [4, 256, 256, 128], P('section', 'row'), may hold values from -6 to 6
- chain_ids: int32 [256], replicated, may hold values from 0 to 2, never falling along the last dimension, each value on 1 to 192 neighbouring positions
- crop_mask: int32 [256], replicated, may hold values 0 or 1
- weight_in: bfloat16 [4, 2, 128, 640], P('section'), may hold values from -0.5 to 0.5
- weight_out: bfloat16 [4, 2, 128, 128], P('section'), may hold values from -0.5 to 0.5
- gain_in: float32 [4, 2, 128], P('section'), may hold values from 0.25 to 1.75
- bias_in: float32 [4, 2, 128], P('section'), may hold values from -3 to 3
- gain_out: float32 [4, 2, 128], P('section'), may hold values from 0.25 to 1.75
- bias_out: float32 [4, 2, 128], P('section'), may hold values from -3 to 3
Outputs:
- next_cotangent: bfloat16 [4, 256, 256, 128], P('section', 'row')
- grad_weight_in: float32 [4, 2, 128, 640], P('section')
- grad_weight_out: float32 [4, 2, 128, 128], P('section')
- grad_norm_in: float32 [4, 2, 2, 128], P('section')
- grad_norm_out: float32 [4, 2, 2, 128], P('section')
The draws below stay inside these ranges and needn't reach their ends.
Inputs may be any that keep to these rules, and one draw needn't show every extreme that they name: `chain_ids`: chain numbers never fall along the residues; the longest chain holds 192 residues. `crop_mask`: 1 marks a residue present in the crop.
All inputs are finite; a program needn't handle non-finite values.
Results may differ from the reference program's by a relative error of at most 0.014.
Values may be sent and summed in bfloat16 or wider, within the bound.
A program may use at most 192 MiB of HBM per device.

```python
import math
import jax
import jax.numpy as jnp
import numpy as np
from jax import lax

C = 128
H = 128
N = 256
CHAINS = 3
N_SECTION = 4


def place_ends(result, own_key, low, top_value):
    longest = result.shape.index(max(result.shape))
    spots = []
    for shift in (0, 1):
        where = [jax.random.randint(jax.random.fold_in(own_key, axis), (), 0, length) for axis, length in enumerate(result.shape)]
        where[longest] = (where[longest] + shift) % result.shape[longest]
        spots.append(tuple(where))
    return result.at[spots[0]].set(low).at[spots[1]].set(top_value)


def block_scale(key, dims, split, low, largest):
    factor_of = 1.0
    for axis_at, shards_of in split:
        draws = jax.random.uniform(jax.random.fold_in(jax.random.fold_in(key, 6), axis_at), (shards_of,), jnp.float32, low / len(split), largest / len(split))
        factor_of = factor_of * jnp.repeat(jnp.exp(draws), dims[axis_at] // shards_of).reshape((-1,) + (1,) * (len(dims) - 1 - axis_at))
    return factor_of


def profile(amount, total, bound, slope):
    loads = [(1 << 20) // math.isqrt(standing ** slope) + 1 for standing in range(2, amount + 1)]
    spare, holding = total - bound - (amount - 1), [1] * (amount - 1)
    while spare > 0:
        free = [i for i in range(amount - 1) if holding[i] < bound]
        mass, budget = sum([loads[i] for i in free]), spare
        for i in free:
            more = min(bound - holding[i], max(1, budget * loads[i] // mass), spare)
            holding[i] = holding[i] + more
            spare = spare - more
    return np.array([bound] + holding)


def uneven(key, count, total, bound, lean):
    if count == 2:
        one = jax.random.randint(key, (), max(1, total - bound), min(bound, total - 1) + 1)
        return jnp.stack([one, total - one])
    sizes = jnp.asarray(profile(count, total, bound, lean), jnp.int32)
    twos = (count - 1) // 2
    source_of, sink = sizes[1:1 + 2 * twos:2], sizes[2:2 + 2 * twos:2]
    room = jnp.minimum(source_of - 1, bound - sink)
    passed = jax.random.randint(jax.random.fold_in(key, 1), (twos,), 0, 1 << 20) % (room + 1)
    sizes = sizes.at[1:1 + 2 * twos:2].set(source_of - passed).at[2:2 + 2 * twos:2].set(sink + passed)
    return sizes[jax.random.permutation(jax.random.fold_in(key, 2), count)]


def gaussian(own_key, shape, spread, most, shards=(), held_as=jnp.bfloat16):
    values = jax.random.normal(own_key, shape, jnp.float32) * spread
    if len(shards) > 0:
        values = block_scale(own_key, shape, shards, -0.22, 0.18) * values
    return jnp.clip(values, min=-most, max=most).astype(held_as)


def setup_inputs(seed: int = 0) -> dict:
    key_list = jax.random.split(jax.random.key(seed), 11)
    return {
        "pair_in": gaussian(key_list[0], (N_SECTION, N, N, C), 1.0, 6.0, ((0, 4), (1, 8))),
        "upstream": gaussian(key_list[1], (N_SECTION, N, N, C), 1.0, 6.0, ((0, 4), (1, 8))),
        "chain_ids": jnp.searchsorted(jnp.cumsum(uneven(key_list[2], CHAINS, N, 3 * N // 4, 2)), jnp.arange(N), side="right").astype(jnp.int32),
        "crop_mask": place_ends((jax.random.randint(key_list[3], (N,), 0, 8) < 7).astype(jnp.int32), jax.random.fold_in(key_list[3], 1), 0, 1),
        "weight_in": gaussian(key_list[4], (N_SECTION, 2, C, 4 * H + C), C ** -0.5, 0.5, ((0, 4),)),
        "weight_out": gaussian(key_list[5], (N_SECTION, 2, H, C), H ** -0.5, 0.5, ((0, 4),)),
        "gain_in": jnp.clip(1.0 + 0.15 * jax.random.normal(key_list[6], (N_SECTION, 2, C), jnp.float32), 0.25, 1.75),
        "bias_in": gaussian(key_list[7], (N_SECTION, 2, C), 0.5, 3.0, ((0, 4),), jnp.float32),
        "gain_out": jnp.clip(1.0 + 0.15 * jax.random.normal(key_list[8], (N_SECTION, 2, H), jnp.float32), 0.25, 1.75),
        "bias_out": gaussian(key_list[9], (N_SECTION, 2, H), 0.5, 3.0, ((0, 4),), jnp.float32),
    }


epsilon = 1e-05

def multiply(pattern, first_part, second):
    return jnp.einsum(pattern, first_part.astype(jnp.float32), second.astype(jnp.float32))

def layer_inputs(pair_rows, pair_mask, weight_inner, gain_inner, bias_inner, hidden):
    values = pair_rows.astype(jnp.float32)
    centered = values - lax.optimization_barrier(jnp.mean(values, axis=-1, keepdims=True))
    inverse_scale = lax.rsqrt(lax.optimization_barrier(jnp.mean(centered * centered, axis=-1, keepdims=True)) + epsilon)
    normal_in = centered * inverse_scale
    normed = (normal_in * gain_inner + bias_inner).astype(jnp.bfloat16)
    projected = multiply('rnc,cf->frn', normed, weight_inner[:, :4 * hidden])
    gating = jax.nn.sigmoid(multiply('rnc,cf->rnf', normed, weight_inner[:, 4 * hidden:]))
    left_sigmoid = jax.nn.sigmoid(projected[:hidden])
    right_sigmoid = jax.nn.sigmoid(projected[2 * hidden:3 * hidden])
    left_edges = (pair_mask * left_sigmoid * projected[hidden:2 * hidden]).astype(jnp.bfloat16)
    right_edges = (pair_mask * right_sigmoid * projected[3 * hidden:]).astype(jnp.bfloat16)
    saved_in = (normal_in, inverse_scale, normed, projected, left_sigmoid, right_sigmoid, gating)
    return (left_edges, right_edges, saved_in)

def triangle_forward(left_edges, right_edges, outgoing):
    if outgoing:
        product = multiply('hik,hjk->hij', left_edges, right_edges)
    else:
        product = multiply('hki,hkj->hij', left_edges, right_edges)
    return product.astype(jnp.bfloat16)

def triangle_backward(grad_product, left_edges, right_edges, outgoing):
    if outgoing:
        grad_leftside = multiply('hij,hjk->hik', grad_product, right_edges)
        grad_rightside = multiply('hij,hik->hjk', grad_product, left_edges)
    else:
        grad_leftside = multiply('hij,hkj->hki', grad_product, right_edges)
        grad_rightside = multiply('hij,hki->hkj', grad_product, left_edges)
    return (grad_leftside.astype(jnp.bfloat16), grad_rightside.astype(jnp.bfloat16))

def layer_output(pair_rows, product, gating, gain_outer, bias_outer, weight_outer):
    values = product.astype(jnp.float32)
    centered = values - lax.optimization_barrier(jnp.mean(values, axis=0, keepdims=True))
    inverse_scale = lax.rsqrt(lax.optimization_barrier(jnp.mean(centered * centered, axis=0, keepdims=True)) + epsilon)
    normal_out = centered * inverse_scale
    normed = (normal_out * gain_outer[:, None, None] + bias_outer[:, None, None]).astype(jnp.bfloat16)
    branch = multiply('hrn,hc->rnc', normed, weight_outer)
    updated = (pair_rows.astype(jnp.float32) + gating * branch).astype(jnp.bfloat16)
    return (updated, (normal_out, inverse_scale, normed, branch))

def output_backward(grad_pair, gating, saved_out, gain_outer, weight_outer):
    normal_out, inverse_scale, normed, branch = saved_out
    upstream_values = grad_pair.astype(jnp.float32)
    grad_branch = (upstream_values * gating).astype(jnp.bfloat16)
    grad_gate = (upstream_values * branch * gating * (1.0 - gating)).astype(jnp.bfloat16)
    grad_weight_out = multiply('hrn,rnc->hc', normed, grad_branch)
    grad_normed = multiply('rnc,hc->hrn', grad_branch, weight_outer)
    grad_gain = lax.optimization_barrier(jnp.sum(grad_normed * normal_out, axis=(1, 2)))
    grad_bias = lax.optimization_barrier(jnp.sum(grad_normed, axis=(1, 2)))
    scaled = grad_normed * gain_outer[:, None, None]
    grad_product = inverse_scale * (scaled - lax.optimization_barrier(jnp.mean(scaled, axis=0, keepdims=True)) - normal_out * lax.optimization_barrier(jnp.mean(scaled * normal_out, axis=0, keepdims=True)))
    return (grad_product.astype(jnp.bfloat16), grad_gate, grad_weight_out, jnp.stack([grad_gain, grad_bias]))

def input_backward(grad_leftside, grad_rightside, grad_gate, saved_in, pair_mask, weight_inner, gain_inner, hidden):
    normal_in, inverse_scale, normed, projected, left_sigmoid, right_sigmoid, gating = saved_in
    left_values = grad_leftside.astype(jnp.float32) * pair_mask
    right_values = grad_rightside.astype(jnp.float32) * pair_mask
    grad_projected = jnp.concatenate([left_values * projected[hidden:2 * hidden] * left_sigmoid * (1.0 - left_sigmoid), left_values * left_sigmoid, right_values * projected[3 * hidden:] * right_sigmoid * (1.0 - right_sigmoid), right_values * right_sigmoid], axis=0).astype(jnp.bfloat16)
    grad_weight_in = jnp.concatenate([multiply('rnc,frn->cf', normed, grad_projected), multiply('rnc,rnf->cf', normed, grad_gate)], axis=1)
    grad_normed = multiply('frn,cf->rnc', grad_projected, weight_inner[:, :4 * hidden]) + multiply('rnf,cf->rnc', grad_gate, weight_inner[:, 4 * hidden:])
    grad_gain = lax.optimization_barrier(jnp.sum(grad_normed * normal_in, axis=(0, 1)))
    grad_bias = lax.optimization_barrier(jnp.sum(grad_normed, axis=(0, 1)))
    scaled = grad_normed * gain_inner
    grad_pair = inverse_scale * (scaled - lax.optimization_barrier(jnp.mean(scaled, axis=-1, keepdims=True)) - normal_in * lax.optimization_barrier(jnp.mean(scaled * normal_in, axis=-1, keepdims=True)))
    return (grad_pair, grad_weight_in, jnp.stack([grad_gain, grad_bias]))

def section_backward(pair_rows, grad_top, pair_mask, weight_inner, weight_outer, gain_inner, bias_inner, gain_outer, bias_outer):
    hidden = weight_outer.shape[1]
    stored = []
    source = pair_rows
    for direction in range(2):
        left_edges, right_edges, saved_in = layer_inputs(source, pair_mask, weight_inner[direction], gain_inner[direction], bias_inner[direction], hidden)
        product = triangle_forward(left_edges, right_edges, direction == 0)
        updated, saved_out = layer_output(source, product, saved_in[6], gain_outer[direction], bias_outer[direction], weight_outer[direction])
        stored.append((left_edges, right_edges, saved_in, saved_out))
        source = updated
    sums_list = [None, None]
    grad_current = grad_top
    branch_grads = [None, None]
    for direction in (1, 0):
        left_edges, right_edges, saved_in, saved_out = stored[direction]
        grad_product, grad_gate, grad_weight_out, grad_norm_out = output_backward(grad_current, saved_in[6], saved_out, gain_outer[direction], weight_outer[direction])
        grad_leftside, grad_rightside = triangle_backward(grad_product, left_edges, right_edges, direction == 0)
        branch_grad, grad_weight_in, grad_norm_in = input_backward(grad_leftside, grad_rightside, grad_gate, saved_in, pair_mask, weight_inner[direction], gain_inner[direction], hidden)
        sums_list[direction] = (grad_weight_in, grad_weight_out, grad_norm_in, grad_norm_out)
        branch_grads[direction] = branch_grad
        if direction == 1:
            grad_current = (grad_top.astype(jnp.float32) + branch_grad).astype(jnp.bfloat16)
    outer_rounded = lax.optimization_barrier(branch_grads[0].astype(jnp.bfloat16))
    grad_input = (grad_current.astype(jnp.float32) + outer_rounded.astype(jnp.float32)).astype(jnp.bfloat16)
    stacked = tuple((jnp.stack([sums_list[0][member], sums_list[1][member]]) for member in range(4)))
    return (grad_input, stacked)

def reference(pair_in, upstream, chain_ids, crop_mask, weight_in, weight_out, gain_in, bias_in, gain_out, bias_out):
    same_chain = chain_ids[:, None] == chain_ids[None, :]
    pair_mask = jnp.where(same_chain, crop_mask[:, None] * crop_mask[None, :], 0).astype(jnp.float32)
    results = []
    for section_index in range(N_SECTION):
        results.append(section_backward(pair_in[section_index], upstream[section_index], pair_mask, weight_in[section_index], weight_out[section_index], gain_in[section_index], bias_in[section_index], gain_out[section_index], bias_out[section_index]))
    inverse_n = 1.0 / N
    next_cotangent = jnp.stack([results[(section_index + 1) % N_SECTION][0] for section_index in range(N_SECTION)])
    grad_weight_in = jnp.stack([results[section_index][1][0] for section_index in range(N_SECTION)]) * inverse_n
    grad_weight_out = jnp.stack([results[section_index][1][1] for section_index in range(N_SECTION)]) * inverse_n
    grad_norm_in = jnp.stack([results[section_index][1][2] for section_index in range(N_SECTION)]) * inverse_n
    grad_norm_out = jnp.stack([results[section_index][1][3] for section_index in range(N_SECTION)]) * inverse_n
    return (next_cotangent, grad_weight_in, grad_weight_out, grad_norm_in, grad_norm_out)
```

```python
import jax
import jax.numpy as jnp
from jax import lax
from jax.sharding import PartitionSpec as P

epsilon = 1e-05


def passed_along(array, axis, by):
    length = lax.axis_size(axis)
    return lax.ppermute(array, axis, [(i, (i + by) % length) for i in range(length)])


def multiply(pattern, first_part, second):
    return jnp.einsum(pattern, first_part, second, preferred_element_type=jnp.float32)


def fold(array):
    quarter = array.shape[-1] // 4
    half = array.shape[0] // 2
    tail = array[..., 2 * quarter : 3 * quarter]
    zeros = jnp.zeros_like(tail)
    kept = array[..., : 2 * quarter] + jnp.concatenate([array[..., 3 * quarter :], zeros], axis=-1)
    return jnp.concatenate([kept[:half], kept[half:], tail[:half], tail[half:]], axis=-1)


def unfold(array, mask):
    quarter = array.shape[-1] // 6

    def one(kept, tail):
        return jnp.concatenate([kept, tail, kept[..., :quarter]], axis=-1)

    both = jnp.concatenate(
        [
            one(array[..., : 2 * quarter], array[..., 4 * quarter : 5 * quarter]),
            one(array[..., 2 * quarter : 4 * quarter], array[..., 5 * quarter :]),
        ],
        axis=0,
    )
    if mask is None:
        return both
    return jnp.where(mask, both, jnp.zeros_like(both))


def to_channels(array, mask):
    moved = lax.all_to_all(fold(array), "row", split_axis=0, concat_axis=1, tiled=True)
    return unfold(moved, mask)


def to_rows(array, mask):
    moved = lax.all_to_all(fold(array), "row", split_axis=1, concat_axis=0, tiled=True)
    return unfold(moved, mask)


def reduced(sums):
    weights_in, weights_out, norm_in, norm_out = sums
    norms = jnp.concatenate([norm_in, norm_out], axis=0)
    columns = weights_out.shape[1]
    norms = jnp.pad(norms, ((0, columns - norms.shape[0]), (0, 0))).T
    flat = jnp.concatenate([weights_in, weights_out, norms], axis=1).astype(jnp.bfloat16)
    width = lax.axis_size("row")
    parts = flat.reshape(width, flat.shape[0] // width, flat.shape[1])
    parts = lax.all_to_all(parts, "row", split_axis=0, concat_axis=0, tiled=True)
    summed = jnp.sum(parts.astype(jnp.float32), axis=0).astype(jnp.bfloat16)
    total = lax.all_gather(summed, "row", axis=0, tiled=True).astype(jnp.float32)
    split = weights_in.shape[1]
    norms = total[:, split + columns : split + columns + 4].T
    return (total[:, :split], total[:, split : split + columns], norms[:2], norms[2:])


def layer_inputs(pair_rows, pair_mask, weight_inner, gain_inner, bias_inner, hidden):
    values = pair_rows.astype(jnp.float32)
    centered = values - jnp.mean(values, axis=-1, keepdims=True)
    inverse_scale = lax.rsqrt(jnp.mean(centered * centered, axis=-1, keepdims=True) + epsilon)
    normal_in = centered * inverse_scale
    normed = (normal_in * gain_inner + bias_inner).astype(jnp.bfloat16)
    projected = multiply("rnc,cf->frn", normed, weight_inner[:, : 4 * hidden])
    gating = jax.nn.sigmoid(multiply("rnc,cf->rnf", normed, weight_inner[:, 4 * hidden :]))
    left_sigmoid = jax.nn.sigmoid(projected[:hidden])
    right_sigmoid = jax.nn.sigmoid(projected[2 * hidden : 3 * hidden])
    left_edges = (pair_mask * left_sigmoid * projected[hidden : 2 * hidden]).astype(jnp.bfloat16)
    right_edges = (pair_mask * right_sigmoid * projected[3 * hidden :]).astype(jnp.bfloat16)
    saved_in = (normal_in, inverse_scale, normed, projected, left_sigmoid, right_sigmoid, gating)
    return (left_edges, right_edges, saved_in)


def triangle_forward(left_edges, right_edges, outgoing):
    if outgoing:
        product = multiply("hik,hjk->hij", left_edges, right_edges)
    else:
        product = multiply("hki,hkj->hij", left_edges, right_edges)
    return product.astype(jnp.bfloat16)


def triangle_backward(grad_product, left_edges, right_edges, outgoing):
    if outgoing:
        grad_leftside = multiply("hij,hjk->hik", grad_product, right_edges)
        grad_rightside = multiply("hij,hik->hjk", grad_product, left_edges)
    else:
        grad_leftside = multiply("hij,hkj->hki", grad_product, right_edges)
        grad_rightside = multiply("hij,hki->hkj", grad_product, left_edges)
    return (grad_leftside.astype(jnp.bfloat16), grad_rightside.astype(jnp.bfloat16))


def layer_output(pair_rows, product, gating, gain_outer, bias_outer, weight_outer):
    values = product.astype(jnp.float32)
    centered = values - jnp.mean(values, axis=0, keepdims=True)
    inverse_scale = lax.rsqrt(jnp.mean(centered * centered, axis=0, keepdims=True) + epsilon)
    normal_out = centered * inverse_scale
    normed = (normal_out * gain_outer[:, None, None] + bias_outer[:, None, None]).astype(
        jnp.bfloat16
    )
    branch = multiply("hrn,hc->rnc", normed, weight_outer)
    updated = (pair_rows.astype(jnp.float32) + gating * branch).astype(jnp.bfloat16)
    return (updated, (normal_out, inverse_scale, normed, branch))


def output_backward(grad_pair, gating, saved_out, gain_outer, weight_outer):
    normal_out, inverse_scale, normed, branch = saved_out
    upstream_values = grad_pair.astype(jnp.float32)
    grad_branch = (upstream_values * gating).astype(jnp.bfloat16)
    grad_gate = (upstream_values * branch * gating * (1.0 - gating)).astype(jnp.bfloat16)
    grad_weight_out = multiply("hrn,rnc->hc", normed, grad_branch)
    grad_normed = multiply("rnc,hc->hrn", grad_branch, weight_outer)
    grad_gain = jnp.sum(grad_normed * normal_out, axis=(1, 2))
    grad_bias = jnp.sum(grad_normed, axis=(1, 2))
    scaled = grad_normed * gain_outer[:, None, None]
    grad_product = inverse_scale * (
        scaled
        - jnp.mean(scaled, axis=0, keepdims=True)
        - normal_out * jnp.mean(scaled * normal_out, axis=0, keepdims=True)
    )
    return (
        grad_product.astype(jnp.bfloat16),
        grad_gate,
        grad_weight_out,
        jnp.stack([grad_gain, grad_bias]),
    )


def input_backward(
    grad_leftside, grad_rightside, grad_gate, saved_in, pair_mask, weight_inner, gain_inner, hidden
):
    normal_in, inverse_scale, normed, projected, left_sigmoid, right_sigmoid, gating = saved_in
    left_values = grad_leftside.astype(jnp.float32) * pair_mask
    right_values = grad_rightside.astype(jnp.float32) * pair_mask
    grad_projected = jnp.concatenate(
        [
            left_values * projected[hidden : 2 * hidden] * left_sigmoid * (1.0 - left_sigmoid),
            left_values * left_sigmoid,
            right_values * projected[3 * hidden :] * right_sigmoid * (1.0 - right_sigmoid),
            right_values * right_sigmoid,
        ],
        axis=0,
    ).astype(jnp.bfloat16)
    grad_weight_in = jnp.concatenate(
        [
            multiply("rnc,frn->cf", normed, grad_projected),
            multiply("rnc,rnf->cf", normed, grad_gate),
        ],
        axis=1,
    )
    grad_normed = multiply("frn,cf->rnc", grad_projected, weight_inner[:, : 4 * hidden]) + multiply(
        "rnf,cf->rnc", grad_gate, weight_inner[:, 4 * hidden :]
    )
    grad_gain = jnp.sum(grad_normed * normal_in, axis=(0, 1))
    grad_bias = jnp.sum(grad_normed, axis=(0, 1))
    scaled = grad_normed * gain_inner
    grad_pair = inverse_scale * (
        scaled
        - jnp.mean(scaled, axis=-1, keepdims=True)
        - normal_in * jnp.mean(scaled * normal_in, axis=-1, keepdims=True)
    )
    return (grad_pair, grad_weight_in, jnp.stack([grad_gain, grad_bias]))


def per_device(
    pair_in,
    upstream,
    chain_ids,
    crop_mask,
    weight_in,
    weight_out,
    gain_in,
    bias_in,
    gain_out,
    bias_out,
):
    row_count = pair_in.shape[1]
    hidden = weight_out.shape[2]
    row_start = lax.axis_index("row") * row_count
    row_chain = lax.dynamic_slice_in_dim(chain_ids, row_start, row_count)
    row_crop = lax.dynamic_slice_in_dim(crop_mask, row_start, row_count)
    same_chain = row_chain[:, None] == chain_ids[None, :]
    pair_mask = jnp.where(same_chain, row_crop[:, None] * crop_mask[None, :], 0).astype(jnp.float32)
    row_mask = pair_mask > 0
    full_mask = (chain_ids[:, None] == chain_ids[None, :]) & (
        (crop_mask[:, None] * crop_mask[None, :]) > 0
    )
    pair_rows = pair_in[0]
    grad_top = upstream[0]

    def forward_update(source, direction, outgoing):
        left_edges, right_edges, saved_in = layer_inputs(
            source,
            pair_mask,
            weight_in[0, direction],
            gain_in[0, direction],
            bias_in[0, direction],
            hidden,
        )
        left_channels = to_channels(left_edges, full_mask)
        right_channels = to_channels(right_edges, full_mask)
        product = to_rows(triangle_forward(left_channels, right_channels, outgoing), row_mask)
        updated, saved_out = layer_output(
            source,
            product,
            saved_in[6],
            gain_out[0, direction],
            bias_out[0, direction],
            weight_out[0, direction],
        )
        return (updated, (left_channels, right_channels, saved_in, saved_out))

    def backward_update(grad_pair, stored, direction, outgoing):
        left_channels, right_channels, saved_in, saved_out = stored
        grad_product, grad_gate, grad_weight_out, grad_norm_out = output_backward(
            grad_pair, saved_in[6], saved_out, gain_out[0, direction], weight_out[0, direction]
        )
        grad_product = jnp.where(row_mask, grad_product, jnp.zeros_like(grad_product))
        grad_channels = to_channels(grad_product, full_mask)
        left_grads, right_grads = triangle_backward(
            grad_channels, left_channels, right_channels, outgoing
        )
        left_grads = jnp.where(full_mask, left_grads, jnp.zeros_like(left_grads))
        right_grads = jnp.where(full_mask, right_grads, jnp.zeros_like(right_grads))
        grad_leftside = to_rows(left_grads, None)
        grad_rightside = to_rows(right_grads, None)
        branch_grad, grad_weight_in, grad_norm_in = input_backward(
            grad_leftside,
            grad_rightside,
            grad_gate,
            saved_in,
            pair_mask,
            weight_in[0, direction],
            gain_in[0, direction],
            hidden,
        )
        return (branch_grad, (grad_weight_in, grad_weight_out, grad_norm_in, grad_norm_out))

    middle, stored_outgoing = forward_update(pair_rows, 0, True)
    top_unused, stored_incoming = forward_update(middle, 1, False)
    grad_inner, sums_incoming = backward_update(grad_top, stored_incoming, 1, False)
    grad_middle = (grad_top.astype(jnp.float32) + grad_inner).astype(jnp.bfloat16)
    grad_outer, sums_outgoing = backward_update(grad_middle, stored_outgoing, 0, True)
    outer_rounded = lax.optimization_barrier(grad_outer.astype(jnp.bfloat16))
    grad_input = (grad_middle.astype(jnp.float32) + outer_rounded.astype(jnp.float32)).astype(
        jnp.bfloat16
    )
    passed_back = passed_along(grad_input, "section", -1)
    incoming_totals = reduced(sums_incoming)
    outgoing_totals = reduced(sums_outgoing)
    totals = [
        jnp.stack([outgoing_totals[member], incoming_totals[member]]) for member in range(4)
    ]
    inverse_n = 1.0 / pair_rows.shape[1]
    return (
        passed_back[None],
        totals[0][None] * inverse_n,
        totals[1][None] * inverse_n,
        totals[2][None] * inverse_n,
        totals[3][None] * inverse_n,
    )


def solution(mesh):
    return jax.shard_map(
        per_device,
        mesh=mesh,
        in_specs=(
            P("section", "row", None, None),
            P("section", "row", None, None),
            P(),
            P(),
            P("section", None, None, None),
            P("section", None, None, None),
            P("section", None, None),
            P("section", None, None),
            P("section", None, None),
            P("section", None, None),
        ),
        out_specs=(
            P("section", "row", None, None),
            P("section", None, None, None),
            P("section", None, None, None),
            P("section", None, None, None),
            P("section", None, None, None),
        ),
        check_vma=False,
    )
```

```python
import jax
import jax.numpy as jnp
from jax import lax
from jax.experimental import pallas as pl
from jax.sharding import PartitionSpec as P

epsilon = 1e-05


def passed_along(array, axis, by):
    length = lax.axis_size(axis)
    return lax.ppermute(array, axis, [(i, (i + by) % length) for i in range(length)])


def multiply(pattern, first_part, second):
    return jnp.einsum(pattern, first_part, second, preferred_element_type=jnp.float32)


def low_lanes(array):
    return lax.broadcasted_iota(jnp.int32, array.shape, 1) < array.shape[1] // 2


def swapped(array):
    half = array.shape[1] // 2
    return jnp.concatenate([array[:, half:], array[:, :half]], axis=1)


def fold_kernel(mask_ref, array_ref, folded_ref):
    half = mask_ref.shape[1] // 2

    @pl.loop(0, folded_ref.shape[1])
    def _(pair):
        tails = []
        for member in range(2):
            if len(array_ref.shape) == 5:
                values = array_ref[member, 0, pair]
            else:
                values = array_ref[member, pair]
            values = values * mask_ref[...]
            first, second = values[:, :half], values[:, half:]
            low = low_lanes(first)
            turned = swapped(second)
            kept = first + jnp.where(low, turned, jnp.zeros_like(turned))
            folded_ref[0, pair, :, member * half : (member + 1) * half] = kept
            tails.append(second if member == 0 else turned)
        folded_ref[0, pair, :, 2 * half :] = jnp.where(low, tails[0], tails[1])


def unfold_kernel(mask_ref, folded_ref, array_ref):
    half = mask_ref.shape[1] // 2

    @pl.loop(0, folded_ref.shape[1])
    def _(pair):
        tail = folded_ref[0, pair, :, 2 * half :]
        low = low_lanes(tail)
        for member in range(2):
            kept = folded_ref[0, pair, :, member * half : (member + 1) * half]
            own = tail if member == 0 else swapped(tail)
            second = jnp.where(low, own, swapped(kept))
            first = kept * mask_ref[:, :half]
            second = second * mask_ref[:, half:]
            if len(array_ref.shape) == 5:
                array_ref[member, 0, pair, :, :half] = first
                array_ref[member, 0, pair, :, half:] = second
            else:
                array_ref[member, pair, :, :half] = first
                array_ref[member, pair, :, half:] = second


def whole_spec(pairs, rows, columns, by_channel):
    if by_channel:
        return pl.BlockSpec((2, 1, pairs, rows, columns), lambda peer: (0, peer, 0, 0, 0))
    return pl.BlockSpec((2, pairs, rows, columns), lambda peer: (0, 0, peer, 0))


def mask_spec(rows, columns, by_channel):
    if by_channel:
        return pl.BlockSpec((rows, columns), lambda peer: (0, 0))
    return pl.BlockSpec((rows, columns), lambda peer: (peer, 0))


def fold(array, mask, by_channel):
    width = lax.axis_size("row")
    columns = array.shape[2]
    if by_channel:
        pairs, rows = array.shape[0] // (2 * width), array.shape[1]
        array = array.reshape(2, width, pairs, rows, columns)
    else:
        pairs, rows = array.shape[0] // 2, array.shape[1] // width
        array = array.reshape(2, pairs, width * rows, columns)
    packed = 3 * (columns // 2)
    return pl.pallas_call(
        fold_kernel,
        grid=(width,),
        in_specs=[
            mask_spec(rows, columns, by_channel),
            whole_spec(pairs, rows, columns, by_channel),
        ],
        out_specs=pl.BlockSpec((1, pairs, rows, packed), lambda peer: (peer, 0, 0, 0)),
        out_shape=jax.ShapeDtypeStruct((width, pairs, rows, packed), array.dtype),
        cost_estimate=pl.CostEstimate(
            flops=array.size * 4, bytes_accessed=array.size * 4, transcendentals=0
        ),
    )(mask, array)


def unfold(moved, mask, by_channel):
    width, pairs, rows, packed = moved.shape
    columns = 2 * (packed // 3)
    if by_channel:
        shape = (2, width, pairs, rows, columns)
    else:
        shape = (2, pairs, width * rows, columns)
    array = pl.pallas_call(
        unfold_kernel,
        grid=(width,),
        in_specs=[
            mask_spec(rows, columns, by_channel),
            pl.BlockSpec((1, pairs, rows, packed), lambda peer: (peer, 0, 0, 0)),
        ],
        out_specs=whole_spec(pairs, rows, columns, by_channel),
        out_shape=jax.ShapeDtypeStruct(shape, moved.dtype),
        cost_estimate=pl.CostEstimate(
            flops=moved.size * 4, bytes_accessed=moved.size * 4, transcendentals=0
        ),
    )(mask, moved)
    if by_channel:
        return array.reshape(2 * width * pairs, rows, columns)
    return array.reshape(2 * pairs, width * rows, columns)


def exchanged(array):
    return lax.all_to_all(array, "row", split_axis=0, concat_axis=0, tiled=True)


def to_channels(array, row_mask, full_mask):
    return unfold(exchanged(fold(array, row_mask, True)), full_mask, False)


def to_rows(array, row_mask, full_mask):
    return unfold(exchanged(fold(array, full_mask, False)), row_mask, True)


def reduced(sums):
    weights_in, weights_out, norm_in, norm_out = sums
    norms = jnp.concatenate([norm_in, norm_out], axis=0)
    columns = weights_out.shape[1]
    norms = jnp.pad(norms, ((0, columns - norms.shape[0]), (0, 0))).T
    flat = jnp.concatenate([weights_in, weights_out, norms], axis=1).astype(jnp.bfloat16)
    width = lax.axis_size("row")
    parts = flat.reshape(width, flat.shape[0] // width, flat.shape[1])
    parts = lax.all_to_all(parts, "row", split_axis=0, concat_axis=0, tiled=True)
    summed = jnp.sum(parts.astype(jnp.float32), axis=0).astype(jnp.bfloat16)
    copies = jnp.broadcast_to(summed[None], (width,) + summed.shape)
    total = exchanged(copies).reshape(flat.shape).astype(jnp.float32)
    split = weights_in.shape[1]
    norms = total[:, split + columns : split + columns + 4].T
    return (total[:, :split], total[:, split : split + columns], norms[:2], norms[2:])


def layer_inputs(pair_rows, pair_mask, weight_inner, gain_inner, bias_inner, hidden):
    values = pair_rows.astype(jnp.float32)
    centered = values - jnp.mean(values, axis=-1, keepdims=True)
    inverse_scale = lax.rsqrt(jnp.mean(centered * centered, axis=-1, keepdims=True) + epsilon)
    normal_in = centered * inverse_scale
    normed = (normal_in * gain_inner + bias_inner).astype(jnp.bfloat16)
    projected = multiply("rnc,cf->frn", normed, weight_inner[:, : 4 * hidden])
    gating = jax.nn.sigmoid(multiply("rnc,cf->rnf", normed, weight_inner[:, 4 * hidden :]))
    left_sigmoid = jax.nn.sigmoid(projected[:hidden])
    right_sigmoid = jax.nn.sigmoid(projected[2 * hidden : 3 * hidden])
    left_edges = (pair_mask * left_sigmoid * projected[hidden : 2 * hidden]).astype(jnp.bfloat16)
    right_edges = (pair_mask * right_sigmoid * projected[3 * hidden :]).astype(jnp.bfloat16)
    saved_in = (normal_in, inverse_scale, normed, projected, left_sigmoid, right_sigmoid, gating)
    return (left_edges, right_edges, saved_in)


def triangle_forward(left_edges, right_edges, outgoing):
    if outgoing:
        product = multiply("hik,hjk->hij", left_edges, right_edges)
    else:
        product = multiply("hki,hkj->hij", left_edges, right_edges)
    return product.astype(jnp.bfloat16)


def triangle_backward(grad_product, left_edges, right_edges, outgoing):
    if outgoing:
        grad_leftside = multiply("hij,hjk->hik", grad_product, right_edges)
        grad_rightside = multiply("hij,hik->hjk", grad_product, left_edges)
    else:
        grad_leftside = multiply("hij,hkj->hki", grad_product, right_edges)
        grad_rightside = multiply("hij,hki->hkj", grad_product, left_edges)
    return (grad_leftside.astype(jnp.bfloat16), grad_rightside.astype(jnp.bfloat16))


def layer_output(pair_rows, product, gating, gain_outer, bias_outer, weight_outer):
    values = product.astype(jnp.float32)
    centered = values - jnp.mean(values, axis=0, keepdims=True)
    inverse_scale = lax.rsqrt(jnp.mean(centered * centered, axis=0, keepdims=True) + epsilon)
    normal_out = centered * inverse_scale
    normed = (normal_out * gain_outer[:, None, None] + bias_outer[:, None, None]).astype(
        jnp.bfloat16
    )
    branch = multiply("hrn,hc->rnc", normed, weight_outer)
    updated = (pair_rows.astype(jnp.float32) + gating * branch).astype(jnp.bfloat16)
    return (updated, (normal_out, inverse_scale, normed, branch))


def output_backward(grad_pair, gating, saved_out, gain_outer, weight_outer):
    normal_out, inverse_scale, normed, branch = saved_out
    upstream_values = grad_pair.astype(jnp.float32)
    grad_branch = (upstream_values * gating).astype(jnp.bfloat16)
    grad_gate = (upstream_values * branch * gating * (1.0 - gating)).astype(jnp.bfloat16)
    grad_weight_out = multiply("hrn,rnc->hc", normed, grad_branch)
    grad_normed = multiply("rnc,hc->hrn", grad_branch, weight_outer)
    grad_gain = jnp.sum(grad_normed * normal_out, axis=(1, 2))
    grad_bias = jnp.sum(grad_normed, axis=(1, 2))
    scaled = grad_normed * gain_outer[:, None, None]
    grad_product = inverse_scale * (
        scaled
        - jnp.mean(scaled, axis=0, keepdims=True)
        - normal_out * jnp.mean(scaled * normal_out, axis=0, keepdims=True)
    )
    return (
        grad_product.astype(jnp.bfloat16),
        grad_gate,
        grad_weight_out,
        jnp.stack([grad_gain, grad_bias]),
    )


def input_backward(
    grad_leftside, grad_rightside, grad_gate, saved_in, pair_mask, weight_inner, gain_inner, hidden
):
    normal_in, inverse_scale, normed, projected, left_sigmoid, right_sigmoid, gating = saved_in
    left_values = grad_leftside.astype(jnp.float32) * pair_mask
    right_values = grad_rightside.astype(jnp.float32) * pair_mask
    grad_projected = jnp.concatenate(
        [
            left_values * projected[hidden : 2 * hidden] * left_sigmoid * (1.0 - left_sigmoid),
            left_values * left_sigmoid,
            right_values * projected[3 * hidden :] * right_sigmoid * (1.0 - right_sigmoid),
            right_values * right_sigmoid,
        ],
        axis=0,
    ).astype(jnp.bfloat16)
    grad_weight_in = jnp.concatenate(
        [
            multiply("rnc,frn->cf", normed, grad_projected),
            multiply("rnc,rnf->cf", normed, grad_gate),
        ],
        axis=1,
    )
    grad_normed = multiply("frn,cf->rnc", grad_projected, weight_inner[:, : 4 * hidden]) + multiply(
        "rnf,cf->rnc", grad_gate, weight_inner[:, 4 * hidden :]
    )
    grad_gain = jnp.sum(grad_normed * normal_in, axis=(0, 1))
    grad_bias = jnp.sum(grad_normed, axis=(0, 1))
    scaled = grad_normed * gain_inner
    grad_pair = inverse_scale * (
        scaled
        - jnp.mean(scaled, axis=-1, keepdims=True)
        - normal_in * jnp.mean(scaled * normal_in, axis=-1, keepdims=True)
    )
    return (grad_pair, grad_weight_in, jnp.stack([grad_gain, grad_bias]))


def per_device(
    pair_in,
    upstream,
    chain_ids,
    crop_mask,
    weight_in,
    weight_out,
    gain_in,
    bias_in,
    gain_out,
    bias_out,
):
    row_count = pair_in.shape[1]
    hidden = weight_out.shape[2]
    row_start = lax.axis_index("row") * row_count
    row_chain = lax.dynamic_slice_in_dim(chain_ids, row_start, row_count)
    row_crop = lax.dynamic_slice_in_dim(crop_mask, row_start, row_count)
    same_chain = row_chain[:, None] == chain_ids[None, :]
    pair_mask = jnp.where(same_chain, row_crop[:, None] * crop_mask[None, :], 0).astype(jnp.float32)
    row_mask = pair_mask.astype(jnp.bfloat16)
    full_mask = jnp.where(
        chain_ids[:, None] == chain_ids[None, :], crop_mask[:, None] * crop_mask[None, :], 0
    ).astype(jnp.bfloat16)
    pair_rows = pair_in[0]
    grad_top = upstream[0]

    def forward_update(source, direction, outgoing):
        left_edges, right_edges, saved_in = layer_inputs(
            source,
            pair_mask,
            weight_in[0, direction],
            gain_in[0, direction],
            bias_in[0, direction],
            hidden,
        )
        left_channels = to_channels(left_edges, row_mask, full_mask)
        right_channels = to_channels(right_edges, row_mask, full_mask)
        product = to_rows(
            triangle_forward(left_channels, right_channels, outgoing), row_mask, full_mask
        )
        updated, saved_out = layer_output(
            source,
            product,
            saved_in[6],
            gain_out[0, direction],
            bias_out[0, direction],
            weight_out[0, direction],
        )
        return (updated, (left_channels, right_channels, saved_in, saved_out))

    def backward_update(grad_pair, stored, direction, outgoing):
        left_channels, right_channels, saved_in, saved_out = stored
        grad_product, grad_gate, grad_weight_out, grad_norm_out = output_backward(
            grad_pair, saved_in[6], saved_out, gain_out[0, direction], weight_out[0, direction]
        )
        grad_channels = to_channels(grad_product, row_mask, full_mask)
        left_grads, right_grads = triangle_backward(
            grad_channels, left_channels, right_channels, outgoing
        )
        grad_leftside = to_rows(left_grads, row_mask, full_mask)
        grad_rightside = to_rows(right_grads, row_mask, full_mask)
        branch_grad, grad_weight_in, grad_norm_in = input_backward(
            grad_leftside,
            grad_rightside,
            grad_gate,
            saved_in,
            pair_mask,
            weight_in[0, direction],
            gain_in[0, direction],
            hidden,
        )
        return (branch_grad, (grad_weight_in, grad_weight_out, grad_norm_in, grad_norm_out))

    middle, stored_outgoing = forward_update(pair_rows, 0, True)
    top_unused, stored_incoming = forward_update(middle, 1, False)
    grad_inner, sums_incoming = backward_update(grad_top, stored_incoming, 1, False)
    grad_middle = (grad_top.astype(jnp.float32) + grad_inner).astype(jnp.bfloat16)
    grad_outer, sums_outgoing = backward_update(grad_middle, stored_outgoing, 0, True)
    outer_rounded = lax.optimization_barrier(grad_outer.astype(jnp.bfloat16))
    grad_input = (grad_middle.astype(jnp.float32) + outer_rounded.astype(jnp.float32)).astype(
        jnp.bfloat16
    )
    passed_back = passed_along(grad_input, "section", -1)
    incoming_totals = reduced(sums_incoming)
    outgoing_totals = reduced(sums_outgoing)
    totals = [
        jnp.stack([outgoing_totals[member], incoming_totals[member]]) for member in range(4)
    ]
    inverse_n = 1.0 / pair_rows.shape[1]
    return (
        passed_back[None],
        totals[0][None] * inverse_n,
        totals[1][None] * inverse_n,
        totals[2][None] * inverse_n,
        totals[3][None] * inverse_n,
    )


def solution(mesh):
    return jax.shard_map(
        per_device,
        mesh=mesh,
        in_specs=(
            P("section", "row", None, None),
            P("section", "row", None, None),
            P(),
            P(),
            P("section", None, None, None),
            P("section", None, None, None),
            P("section", None, None),
            P("section", None, None),
            P("section", None, None),
            P("section", None, None),
        ),
        out_specs=(
            P("section", "row", None, None),
            P("section", None, None, None),
            P("section", None, None, None),
            P("section", None, None, None),
            P("section", None, None, None),
        ),
        check_vma=False,
    )
```

```python
import functools

import jax
import jax.numpy as jnp
from jax import lax
from jax.experimental import pallas as pl
from jax.experimental.pallas import tpu as pltpu
from jax.sharding import PartitionSpec as P

epsilon = 1e-05


def passed_along(array, axis, by):
    length = lax.axis_size(axis)
    return lax.ppermute(array, axis, [(i, (i + by) % length) for i in range(length)])


def multiply(pattern, first_part, second):
    return jnp.einsum(pattern, first_part, second, preferred_element_type=jnp.float32)


def low_lanes(array):
    return lax.broadcasted_iota(jnp.int32, array.shape, 1) < array.shape[1] // 2


def swapped(array):
    half = array.shape[1] // 2
    return jnp.concatenate([array[:, half:], array[:, :half]], axis=1)


def fold_kernel(mask_ref, array_ref, folded_ref):
    half = mask_ref.shape[1] // 2

    for pair in range(folded_ref.shape[1]):
        tails = []
        for member in range(2):
            values = array_ref[member, 0, pair] * mask_ref[...]
            first, second = values[:, :half], values[:, half:]
            low = low_lanes(first)
            turned = swapped(second)
            kept = first + jnp.where(low, turned, jnp.zeros_like(turned))
            folded_ref[0, pair, :, member * half : (member + 1) * half] = kept
            tails.append(second if member == 0 else turned)
        folded_ref[0, pair, :, 2 * half :] = jnp.where(low, tails[0], tails[1])


def unfold_kernel(mask_ref, folded_ref, array_ref):
    half = mask_ref.shape[1] // 2

    for pair in range(folded_ref.shape[1]):
        tail = folded_ref[0, pair, :, 2 * half :]
        low = low_lanes(tail)
        for member in range(2):
            kept = folded_ref[0, pair, :, member * half : (member + 1) * half]
            own = tail if member == 0 else swapped(tail)
            second = jnp.where(low, own, swapped(kept))
            first = kept * mask_ref[:, :half]
            second = second * mask_ref[:, half:]
            array_ref[member, 0, pair, :, :half] = first
            array_ref[member, 0, pair, :, half:] = second


def fold(array, mask):
    width = lax.axis_size("row")
    pairs, rows, columns = array.shape[0] // (2 * width), array.shape[1], array.shape[2]
    packed = 3 * (columns // 2)
    return pl.pallas_call(
        fold_kernel,
        grid=(width,),
        in_specs=[
            pl.BlockSpec((rows, columns), lambda peer: (0, 0)),
            pl.BlockSpec((2, 1, pairs, rows, columns), lambda peer: (0, peer, 0, 0, 0)),
        ],
        out_specs=pl.BlockSpec((1, pairs, rows, packed), lambda peer: (peer, 0, 0, 0)),
        out_shape=jax.ShapeDtypeStruct((width, pairs, rows, packed), array.dtype),
        cost_estimate=pl.CostEstimate(
            flops=array.size * 4, bytes_accessed=array.size * 4, transcendentals=0
        ),
    )(mask, array.reshape(2, width, pairs, rows, columns))


def unfold(moved, mask):
    width, pairs, rows, packed = moved.shape
    columns = 2 * (packed // 3)
    array = pl.pallas_call(
        unfold_kernel,
        grid=(width,),
        in_specs=[
            pl.BlockSpec((rows, columns), lambda peer: (0, 0)),
            pl.BlockSpec((1, pairs, rows, packed), lambda peer: (peer, 0, 0, 0)),
        ],
        out_specs=pl.BlockSpec((2, 1, pairs, rows, columns), lambda peer: (0, peer, 0, 0, 0)),
        out_shape=jax.ShapeDtypeStruct((2, width, pairs, rows, columns), moved.dtype),
        cost_estimate=pl.CostEstimate(
            flops=moved.size * 4, bytes_accessed=moved.size * 4, transcendentals=0
        ),
    )(mask, moved)
    return array.reshape(2 * width * pairs, rows, columns)


def exchanged(array):
    return lax.all_to_all(array, "row", split_axis=0, concat_axis=0, tiled=True)


def to_channels(array, row_mask):
    return exchanged(fold(array, row_mask))


def to_rows(folded, row_mask):
    return unfold(exchanged(folded), row_mask)


def read_pair(ref):
    peers, _, rows, packed = ref.shape
    folded = ref[:, 0]
    if rows % 16:
        folded = folded.astype(jnp.float32)
    return folded.reshape(peers * rows, packed).astype(jnp.bfloat16)


def write_pair(ref, members, mask):
    peers, _, rows, packed = ref.shape
    half = packed // 3
    kept, tails = [], []
    for member, values in enumerate(members):
        values = values.astype(jnp.bfloat16) * mask
        first, second = values[:, :half], values[:, half:]
        low = low_lanes(first)
        turned = swapped(second)
        kept.append(first + jnp.where(low, turned, jnp.zeros_like(turned)))
        tails.append(second if member == 0 else turned)
    folded = jnp.concatenate(kept + [jnp.where(low, tails[0], tails[1])], axis=1)
    if rows % 16:
        folded = folded.astype(jnp.float32)
    ref[:, 0] = folded.reshape(peers, rows, packed).astype(jnp.bfloat16)


def member_of(folded, member, mask):
    half = folded.shape[1] // 3
    tail = folded[:, 2 * half :]
    kept = folded[:, member * half : (member + 1) * half]
    own = tail if member == 0 else swapped(tail)
    second = jnp.where(low_lanes(tail), own, swapped(kept))
    return jnp.concatenate([kept, second], axis=1) * mask


def contracted(first, second, first_axis, second_axis):
    return lax.dot_general(
        first,
        second,
        (((first_axis,), (second_axis,)), ((), ())),
        preferred_element_type=jnp.float32,
    )


def forward_kernel(outgoing, mask_ref, left_ref, right_ref, product_ref):
    mask = mask_ref[...]
    left_pair, right_pair = read_pair(left_ref), read_pair(right_ref)
    members = []
    for member in range(2):
        left_edges = member_of(left_pair, member, mask)
        right_edges = member_of(right_pair, member, mask)
        axis = 1 if outgoing else 0
        members.append(contracted(left_edges, right_edges, axis, axis))
    write_pair(product_ref, members, mask)


def backward_kernel(
    outgoing, mask_ref, grad_ref, left_ref, right_ref, left_grad_ref, right_grad_ref
):
    mask = mask_ref[...]
    grad_pair = read_pair(grad_ref)
    left_pair, right_pair = read_pair(left_ref), read_pair(right_ref)
    left_grads, right_grads = [], []
    for member in range(2):
        grad = member_of(grad_pair, member, mask)
        left_edges = member_of(left_pair, member, mask)
        right_edges = member_of(right_pair, member, mask)
        if outgoing:
            left_grads.append(contracted(grad, right_edges, 1, 0))
            right_grads.append(contracted(grad, left_edges, 0, 0))
        else:
            left_grads.append(contracted(right_edges, grad, 1, 1))
            right_grads.append(contracted(left_edges, grad, 1, 0))
    write_pair(left_grad_ref, left_grads, mask)
    write_pair(right_grad_ref, right_grads, mask)


def triangle(kernel, outgoing, outputs, mask, *operands):
    peers, pairs, rows, packed = operands[0].shape
    block = pl.BlockSpec((peers, 1, rows, packed), lambda pair: (0, pair, 0, 0))
    shape = jax.ShapeDtypeStruct(operands[0].shape, operands[0].dtype)
    residues = mask.shape[0]
    return pl.pallas_call(
        functools.partial(kernel, outgoing),
        grid=(pairs,),
        in_specs=[pl.BlockSpec(mask.shape, lambda pair: (0, 0))] + [block] * len(operands),
        out_specs=[block] * outputs,
        out_shape=[shape] * outputs,
        cost_estimate=pl.CostEstimate(
            flops=4 * outputs * pairs * residues**3,
            bytes_accessed=2 * operands[0].size * (len(operands) + outputs),
            transcendentals=0,
        ),
        compiler_params=pltpu.CompilerParams(vmem_limit_bytes=32 * 1024 * 1024),
    )(mask, *operands)


def reduced(sums):
    weights_in, weights_out, norm_in, norm_out = sums
    norms = jnp.concatenate([norm_in, norm_out], axis=0)
    columns = weights_out.shape[1]
    norms = jnp.pad(norms, ((0, columns - norms.shape[0]), (0, 0))).T
    flat = jnp.concatenate([weights_in, weights_out, norms], axis=1).astype(jnp.bfloat16)
    width = lax.axis_size("row")
    parts = flat.reshape(width, flat.shape[0] // width, flat.shape[1])
    parts = lax.all_to_all(parts, "row", split_axis=0, concat_axis=0, tiled=True)
    summed = jnp.sum(parts.astype(jnp.float32), axis=0).astype(jnp.bfloat16)
    copies = jnp.broadcast_to(summed[None], (width,) + summed.shape)
    total = exchanged(copies).reshape(flat.shape).astype(jnp.float32)
    split = weights_in.shape[1]
    norms = total[:, split + columns : split + columns + 4].T
    return (total[:, :split], total[:, split : split + columns], norms[:2], norms[2:])


def layer_inputs(pair_rows, pair_mask, weight_inner, gain_inner, bias_inner, hidden):
    values = pair_rows.astype(jnp.float32)
    centered = values - jnp.mean(values, axis=-1, keepdims=True)
    inverse_scale = lax.rsqrt(jnp.mean(centered * centered, axis=-1, keepdims=True) + epsilon)
    normal_in = centered * inverse_scale
    normed = (normal_in * gain_inner + bias_inner).astype(jnp.bfloat16)
    projected = multiply("rnc,cf->frn", normed, weight_inner[:, : 4 * hidden])
    gating = jax.nn.sigmoid(multiply("rnc,cf->rnf", normed, weight_inner[:, 4 * hidden :]))
    left_sigmoid = jax.nn.sigmoid(projected[:hidden])
    right_sigmoid = jax.nn.sigmoid(projected[2 * hidden : 3 * hidden])
    left_edges = (pair_mask * left_sigmoid * projected[hidden : 2 * hidden]).astype(jnp.bfloat16)
    right_edges = (pair_mask * right_sigmoid * projected[3 * hidden :]).astype(jnp.bfloat16)
    saved_in = (normal_in, inverse_scale, normed, projected, left_sigmoid, right_sigmoid, gating)
    return (left_edges, right_edges, saved_in)


def layer_output(pair_rows, product, gating, gain_outer, bias_outer, weight_outer):
    values = product.astype(jnp.float32)
    centered = values - jnp.mean(values, axis=0, keepdims=True)
    inverse_scale = lax.rsqrt(jnp.mean(centered * centered, axis=0, keepdims=True) + epsilon)
    normal_out = centered * inverse_scale
    normed = (normal_out * gain_outer[:, None, None] + bias_outer[:, None, None]).astype(
        jnp.bfloat16
    )
    branch = multiply("hrn,hc->rnc", normed, weight_outer)
    updated = (pair_rows.astype(jnp.float32) + gating * branch).astype(jnp.bfloat16)
    return (updated, (normal_out, inverse_scale, normed, branch))


def output_backward(grad_pair, gating, saved_out, gain_outer, weight_outer):
    normal_out, inverse_scale, normed, branch = saved_out
    upstream_values = grad_pair.astype(jnp.float32)
    grad_branch = (upstream_values * gating).astype(jnp.bfloat16)
    grad_gate = (upstream_values * branch * gating * (1.0 - gating)).astype(jnp.bfloat16)
    grad_weight_out = multiply("hrn,rnc->hc", normed, grad_branch)
    grad_normed = multiply("rnc,hc->hrn", grad_branch, weight_outer)
    grad_gain = jnp.sum(grad_normed * normal_out, axis=(1, 2))
    grad_bias = jnp.sum(grad_normed, axis=(1, 2))
    scaled = grad_normed * gain_outer[:, None, None]
    grad_product = inverse_scale * (
        scaled
        - jnp.mean(scaled, axis=0, keepdims=True)
        - normal_out * jnp.mean(scaled * normal_out, axis=0, keepdims=True)
    )
    return (
        grad_product.astype(jnp.bfloat16),
        grad_gate,
        grad_weight_out,
        jnp.stack([grad_gain, grad_bias]),
    )


def input_backward(
    grad_leftside, grad_rightside, grad_gate, saved_in, pair_mask, weight_inner, gain_inner, hidden
):
    normal_in, inverse_scale, normed, projected, left_sigmoid, right_sigmoid, gating = saved_in
    left_values = grad_leftside.astype(jnp.float32) * pair_mask
    right_values = grad_rightside.astype(jnp.float32) * pair_mask
    grad_projected = jnp.concatenate(
        [
            left_values * projected[hidden : 2 * hidden] * left_sigmoid * (1.0 - left_sigmoid),
            left_values * left_sigmoid,
            right_values * projected[3 * hidden :] * right_sigmoid * (1.0 - right_sigmoid),
            right_values * right_sigmoid,
        ],
        axis=0,
    ).astype(jnp.bfloat16)
    grad_weight_in = jnp.concatenate(
        [
            multiply("rnc,frn->cf", normed, grad_projected),
            multiply("rnc,rnf->cf", normed, grad_gate),
        ],
        axis=1,
    )
    grad_normed = multiply("frn,cf->rnc", grad_projected, weight_inner[:, : 4 * hidden]) + multiply(
        "rnf,cf->rnc", grad_gate, weight_inner[:, 4 * hidden :]
    )
    grad_gain = jnp.sum(grad_normed * normal_in, axis=(0, 1))
    grad_bias = jnp.sum(grad_normed, axis=(0, 1))
    scaled = grad_normed * gain_inner
    grad_pair = inverse_scale * (
        scaled
        - jnp.mean(scaled, axis=-1, keepdims=True)
        - normal_in * jnp.mean(scaled * normal_in, axis=-1, keepdims=True)
    )
    return (grad_pair, grad_weight_in, jnp.stack([grad_gain, grad_bias]))


def per_device(
    pair_in,
    upstream,
    chain_ids,
    crop_mask,
    weight_in,
    weight_out,
    gain_in,
    bias_in,
    gain_out,
    bias_out,
):
    row_count = pair_in.shape[1]
    hidden = weight_out.shape[2]
    row_start = lax.axis_index("row") * row_count
    row_chain = lax.dynamic_slice_in_dim(chain_ids, row_start, row_count)
    row_crop = lax.dynamic_slice_in_dim(crop_mask, row_start, row_count)
    same_chain = row_chain[:, None] == chain_ids[None, :]
    pair_mask = jnp.where(same_chain, row_crop[:, None] * crop_mask[None, :], 0).astype(jnp.float32)
    row_mask = pair_mask.astype(jnp.bfloat16)
    full_mask = jnp.where(
        chain_ids[:, None] == chain_ids[None, :], crop_mask[:, None] * crop_mask[None, :], 0
    ).astype(jnp.bfloat16)
    pair_rows = pair_in[0]
    grad_top = upstream[0]

    def forward_update(source, direction, outgoing):
        left_edges, right_edges, saved_in = layer_inputs(
            source,
            pair_mask,
            weight_in[0, direction],
            gain_in[0, direction],
            bias_in[0, direction],
            hidden,
        )
        left_channels = to_channels(left_edges, row_mask)
        right_channels = to_channels(right_edges, row_mask)
        (folded,) = triangle(
            forward_kernel, outgoing, 1, full_mask, left_channels, right_channels
        )
        product = to_rows(folded, row_mask)
        updated, saved_out = layer_output(
            source,
            product,
            saved_in[6],
            gain_out[0, direction],
            bias_out[0, direction],
            weight_out[0, direction],
        )
        return (updated, (left_channels, right_channels, saved_in, saved_out))

    def backward_update(grad_pair, stored, direction, outgoing):
        left_channels, right_channels, saved_in, saved_out = stored
        grad_product, grad_gate, grad_weight_out, grad_norm_out = output_backward(
            grad_pair, saved_in[6], saved_out, gain_out[0, direction], weight_out[0, direction]
        )
        grad_channels = to_channels(grad_product, row_mask)
        left_grads, right_grads = triangle(
            backward_kernel, outgoing, 2, full_mask, grad_channels, left_channels, right_channels
        )
        grad_leftside = to_rows(left_grads, row_mask)
        grad_rightside = to_rows(right_grads, row_mask)
        branch_grad, grad_weight_in, grad_norm_in = input_backward(
            grad_leftside,
            grad_rightside,
            grad_gate,
            saved_in,
            pair_mask,
            weight_in[0, direction],
            gain_in[0, direction],
            hidden,
        )
        return (branch_grad, (grad_weight_in, grad_weight_out, grad_norm_in, grad_norm_out))

    middle, stored_outgoing = forward_update(pair_rows, 0, True)
    top_unused, stored_incoming = forward_update(middle, 1, False)
    grad_inner, sums_incoming = backward_update(grad_top, stored_incoming, 1, False)
    grad_middle = (grad_top.astype(jnp.float32) + grad_inner).astype(jnp.bfloat16)
    grad_outer, sums_outgoing = backward_update(grad_middle, stored_outgoing, 0, True)
    outer_rounded = lax.optimization_barrier(grad_outer.astype(jnp.bfloat16))
    grad_input = (grad_middle.astype(jnp.float32) + outer_rounded.astype(jnp.float32)).astype(
        jnp.bfloat16
    )
    passed_back = passed_along(grad_input, "section", -1)
    incoming_totals = reduced(sums_incoming)
    outgoing_totals = reduced(sums_outgoing)
    totals = [
        jnp.stack([outgoing_totals[member], incoming_totals[member]]) for member in range(4)
    ]
    inverse_n = 1.0 / pair_rows.shape[1]
    return (
        passed_back[None],
        totals[0][None] * inverse_n,
        totals[1][None] * inverse_n,
        totals[2][None] * inverse_n,
        totals[3][None] * inverse_n,
    )


def solution(mesh):
    return jax.shard_map(
        per_device,
        mesh=mesh,
        in_specs=(
            P("section", "row", None, None),
            P("section", "row", None, None),
            P(),
            P(),
            P("section", None, None, None),
            P("section", None, None, None),
            P("section", None, None),
            P("section", None, None),
            P("section", None, None),
            P("section", None, None),
        ),
        out_specs=(
            P("section", "row", None, None),
            P("section", None, None, None),
            P("section", None, None, None),
            P("section", None, None, None),
            P("section", None, None, None),
        ),
        check_vma=False,
    )
```
